32 devices in a mesh: dp: 4 (over y, x), section: 2 (over core), tensor: 4 (over z).
Axes of the slice: x: 2, y: 2, z: 4, core: 2. Of those that a mesh axis runs over, the one named last changes fastest.
Arguments:
- fwd_state: bfloat16 [2, 512, 4096], P('section', ('dp', 'tensor')), may hold values from -6 to 6
- bwd_state: bfloat16 [2, 512, 4096], P('section', ('dp', 'tensor')), may hold values from -6 to 6
- stash: bfloat16 [2, 2, 512, 4096], P('section', None, ('dp', 'tensor')), may hold values from -6 to 6
- gains: bfloat16 [2, 2, 4096], P('section'), may hold values from 0.25 to 1.75
- w_query: bfloat16 [2, 2, 4096, 4096], P('section', None, 'dp', 'tensor'), may hold values from -0.09375 to 0.09375
- w_key: bfloat16 [2, 2, 4096, 1024], P('section', None, 'dp', 'tensor'), may hold values from -0.09375 to 0.09375
- w_value: bfloat16 [2, 2, 4096, 1024], P('section', None, 'dp', 'tensor'), may hold values from -0.09375 to 0.09375
- w_out: bfloat16 [2, 2, 4096, 4096], P('section', None, 'tensor', 'dp'), may hold values from -0.09375 to 0.09375
- fwd_segments: int32 [2, 4, 128], P(None, 'dp'), may hold values from 0 to 3, never falling along the last dimension, each value on 1 to 64 neighbouring positions
- bwd_segments: int32 [2, 4, 128], P(None, 'dp'), may hold values from 0 to 3, never falling along the last dimension, each value on 1 to 64 neighbouring positions
Outputs:
- fwd_out: bfloat16 [2, 512, 4096], P('section', ('dp', 'tensor'))
- bwd_out: bfloat16 [2, 512, 4096], P('section', ('dp', 'tensor'))
- gain_grad: float32 [2, 2, 4096], P('section')
The draws below stay inside these ranges and needn't reach their ends.
Inputs may be any that keep to these rules, and one draw needn't show every extreme that they name: `fwd_segments`: in each replica's rows of each micro-batch the document ids never fall; each document has at most 64 rows and one has exactly that many. `bwd_segments`: in each replica's rows of each micro-batch the document ids never fall; each document has at most 64 rows and one has exactly that many.
All inputs are finite; a program needn't handle non-finite values.
Results may differ from the reference program's by a relative error of at most 0.02.
Values may be sent and summed in bfloat16 or wider, within the bound.
A program may use at most 192 MiB of HBM per device.

```python
import math
import jax
import jax.numpy as jnp
import numpy as np
from jax import lax

D = 4096
HEADS = 32
KV = 8
HD = 128
R = 128
TICKS = 2
SECTIONS = 2
REPLICAS = 4
ROWS = 512
N_DP = 4
N_SECTION = 2
N_TENSOR = 4


def steps_of(rng, extent, shards, least, largest):
    def one(axis_at, blocks):
        steps = jax.random.uniform(jax.random.fold_in(jax.random.fold_in(rng, 6), axis_at), (blocks,), jnp.float32, least / len(shards), largest / len(shards))
        return jnp.repeat(jnp.exp(steps), extent[axis_at] // blocks).reshape((-1,) + (1,) * (len(extent) - axis_at - 1))

    level = one(*shards[0])
    for cut in shards[1:]:
        level = level * one(*cut)
    return level


def profile(amount, total, limit, lean):
    loads = [(1 << 20) // math.isqrt(rank ** lean) + 1 for rank in range(2, amount + 1)]
    rest, counts = total - limit - (amount - 1), [1] * (amount - 1)
    while rest > 0:
        movable = [i for i in range(amount - 1) if counts[i] < limit]
        pool, budget = sum([loads[i] for i in movable]), rest
        for i in movable:
            more = min(limit - counts[i], max(1, budget * loads[i] // pool), rest)
            counts[i] = counts[i] + more
            rest = rest - more
    return np.array([limit] + counts)


def ragged(own_key, count, total, reach, skew):
    if count == 2:
        one = jax.random.randint(own_key, (), max(1, total - reach), min(reach, total - 1) + 1)
        return jnp.stack([one, total - one])
    lengths = jnp.asarray(profile(count, total, reach, skew), jnp.int32)
    twos = (count - 1) // 2
    giver, taker = lengths[1:1 + 2 * twos:2], lengths[2:2 + 2 * twos:2]
    room = jnp.minimum(giver - 1, reach - taker)
    passed = jax.random.randint(jax.random.fold_in(own_key, 1), (twos,), 0, 1 << 20) % (room + 1)
    lengths = lengths.at[1:1 + 2 * twos:2].set(giver - passed).at[2:2 + 2 * twos:2].set(taker + passed)
    return lengths[jax.random.permutation(jax.random.fold_in(own_key, 2), count)]


def normal_values(key, extent, spread, reach, shards=(), kind=jnp.bfloat16):
    factor_of = steps_of(key, extent, shards, -0.22, 0.18) if shards else 1.0
    result = jax.random.normal(key, extent, jnp.float32) * spread * factor_of
    return jnp.minimum(jnp.maximum(result, -reach), reach).astype(kind)


def setup_inputs(seed: int = 0) -> dict:
    keys = jax.random.split(jax.random.key(seed), 11)
    return {
        "fwd_state": normal_values(keys[0], (SECTIONS, ROWS, D), 1.0, 6.0, ((0, 2), (1, 16))),
        "bwd_state": normal_values(keys[1], (SECTIONS, ROWS, D), 1.0, 6.0, ((0, 2), (1, 16))),
        "stash": normal_values(keys[2], (SECTIONS, TICKS, ROWS, D), 1.0, 6.0, ((0, 2), (2, 16))),
        "gains": jnp.clip(1.0 + 0.15 * jax.random.normal(keys[3], (SECTIONS, 2, D), jnp.float32), 0.25, 1.75).astype(jnp.bfloat16),
        "w_query": normal_values(keys[4], (SECTIONS, 2, D, HEADS * HD), D ** -0.5, 0.09375, ((0, 2), (2, 4), (3, 4))),
        "w_key": normal_values(keys[5], (SECTIONS, 2, D, KV * HD), D ** -0.5, 0.09375, ((0, 2), (2, 4), (3, 4))),
        "w_value": normal_values(keys[6], (SECTIONS, 2, D, KV * HD), D ** -0.5, 0.09375, ((0, 2), (2, 4), (3, 4))),
        "w_out": normal_values(keys[7], (SECTIONS, 2, HEADS * HD, D), (HEADS * HD) ** -0.5, 0.09375, ((0, 2), (2, 4), (3, 4))),
        "fwd_segments": jax.vmap(lambda own: jnp.searchsorted(jnp.cumsum(ragged(own, 4, R, R // 2, 0)), jnp.arange(R), side="right"))(jax.random.split(keys[8], SECTIONS * REPLICAS)).reshape((SECTIONS, REPLICAS, R)).astype(jnp.int32),
        "bwd_segments": jax.vmap(lambda own: jnp.searchsorted(jnp.cumsum(ragged(own, 4, R, R // 2, 0)), jnp.arange(R), side="right"))(jax.random.split(keys[9], SECTIONS * REPLICAS)).reshape((SECTIONS, REPLICAS, R)).astype(jnp.int32),
    }


ROPE_BASE = 1000000.0

def rope_tables(segments):
    count_rows = segments.shape[0]
    row_index = jnp.arange(count_rows, dtype=jnp.int32)
    previous = jnp.concatenate([segments[:1] - 1, segments[:-1]])
    doc_starts = lax.cummax(jnp.where(segments != previous, row_index, 0), axis=0)
    positions = (row_index - doc_starts).astype(jnp.float32)
    halfway = HD // 2
    frequency = jnp.exp(jnp.arange(halfway, dtype=jnp.float32) * (-2.0 * math.log(ROPE_BASE) / HD))
    angles = positions[:, None] * frequency[None, :]
    cosine = jnp.concatenate([jnp.cos(angles), jnp.cos(angles)], axis=1)
    sine_table = jnp.concatenate([jnp.sin(angles), jnp.sin(angles)], axis=1)
    allowed = (segments[:, None] == segments[None, :]) & (row_index[:, None] >= row_index[None, :])
    return (cosine[:, None, :], sine_table[:, None, :], allowed)

def rotate(vectors, cosine, sine_table):
    halfway = vectors.shape[-1] // 2
    turned = jnp.concatenate([-vectors[..., halfway:], vectors[..., :halfway]], axis=-1)
    return vectors * cosine + turned * sine_table

def partial_layer(state_rows, gain_vector, w_query, w_key, w_value, w_out, segments):
    count_rows = state_rows.shape[0]
    cosine, sine_table, allowed = rope_tables(segments)
    variance = lax.optimization_barrier(jnp.mean(state_rows * state_rows, axis=1, keepdims=True))
    normed = (state_rows * lax.rsqrt(variance + 1e-06) * gain_vector).astype(jnp.bfloat16)
    query_rows = jnp.dot(normed, w_query, preferred_element_type=jnp.float32).reshape(count_rows, -1, HD)
    key_rows = jnp.dot(normed, w_key, preferred_element_type=jnp.float32).reshape(count_rows, -1, HD)
    value_rows = jnp.dot(normed, w_value, preferred_element_type=jnp.float32).astype(jnp.bfloat16)
    value_rows = value_rows.reshape(count_rows, -1, HD)
    query_rows = rotate(query_rows, cosine, sine_table).astype(jnp.bfloat16)
    key_rows = rotate(key_rows, cosine, sine_table).astype(jnp.bfloat16)
    key_heads = key_rows.shape[1]
    grouped = query_rows.reshape(count_rows, key_heads, -1, HD)
    scores = jnp.einsum('qkgd,skd->kgqs', grouped.astype(jnp.float32), key_rows.astype(jnp.float32))
    scores = scores * (1.0 / math.sqrt(HD))
    scores = jnp.where(allowed[None, None], scores, -1e+30)
    exponents = jnp.exp(scores)
    soft_weights = (exponents / lax.optimization_barrier(jnp.sum(exponents, axis=-1, keepdims=True))).astype(jnp.bfloat16)
    mixed_heads = jnp.einsum('kgqs,skd->qkgd', soft_weights.astype(jnp.float32), value_rows.astype(jnp.float32))
    mixed_heads = mixed_heads.astype(jnp.bfloat16).reshape(count_rows, -1)
    return jnp.dot(mixed_heads, w_out, preferred_element_type=jnp.float32)

def round_trip(terms):
    return lax.optimization_barrier(terms.astype(jnp.bfloat16)).astype(jnp.float32)

def pick_span(table, span):
    return lax.dynamic_index_in_dim(table, span, 0, keepdims=False)

def split_groups(w_query, w_key, w_value, w_out, span):
    query_pick = pick_span(w_query, span)
    key_pick = pick_span(w_key, span)
    value_pick = pick_span(w_value, span)
    out_pick = pick_span(w_out, span)
    model_width = query_pick.shape[0]
    return (query_pick.reshape(model_width, N_TENSOR, -1).transpose(1, 0, 2), key_pick.reshape(model_width, N_TENSOR, -1).transpose(1, 0, 2), value_pick.reshape(model_width, N_TENSOR, -1).transpose(1, 0, 2), out_pick.reshape(N_TENSOR, -1, model_width))

def phase_forward(operands):
    state_block, gains, w_query, w_key, w_value, w_out, span, segments = operands
    gain_vector = pick_span(gains, span).astype(jnp.float32)
    group_query, group_key, group_value, group_out = split_groups(w_query, w_key, w_value, w_out, span)

    def one_replica(rows_in, segment_row):

        def one_group(query_part, key_part, value_part, out_part):
            return partial_layer(rows_in.astype(jnp.float32), gain_vector, query_part, key_part, value_part, out_part, segment_row)
        terms = jax.vmap(one_group)(group_query, group_key, group_value, group_out)
        return lax.optimization_barrier(jnp.sum(round_trip(terms), axis=0))
    summed = jax.vmap(one_replica)(state_block, segments)
    return (state_block.astype(jnp.float32) + summed).astype(jnp.bfloat16)

def phase_backward(operands):
    stash_block, cotangent, gains, w_query, w_key, w_value, w_out, span, segments = operands
    gain_vector = pick_span(gains, span).astype(jnp.float32)
    group_query, group_key, group_value, group_out = split_groups(w_query, w_key, w_value, w_out, span)

    def one_replica(rows_in, cot_rows, segment_row):

        def one_group(query_part, key_part, value_part, out_part):

            def local(state_in, gain_in):
                return partial_layer(state_in, gain_in, query_part, key_part, value_part, out_part, segment_row)
            unused, pull = jax.vjp(local, rows_in.astype(jnp.float32), gain_vector)
            return pull(cot_rows.astype(jnp.float32))
        state_terms, gain_terms = jax.vmap(one_group)(group_query, group_key, group_value, group_out)
        return (lax.optimization_barrier(jnp.sum(round_trip(state_terms), axis=0)), lax.optimization_barrier(jnp.sum(gain_terms, axis=0)))
    row_terms, gain_terms = jax.vmap(one_replica)(stash_block, cotangent, segments)
    returned = (cotangent.astype(jnp.float32) + row_terms).astype(jnp.bfloat16)
    return (returned, lax.optimization_barrier(jnp.sum(gain_terms, axis=0)))

def reference(fwd_state, bwd_state, stash, gains, w_query, w_key, w_value, w_out, fwd_segments, bwd_segments):
    model_width = fwd_state.shape[2]
    forward_blocks = fwd_state.reshape(N_SECTION, N_DP, R, model_width)
    backward_blocks = bwd_state.reshape(N_SECTION, N_DP, R, model_width)
    stash_blocks = stash.reshape(N_SECTION, TICKS, N_DP, R, model_width)
    phase_ids = jnp.arange(N_SECTION, dtype=jnp.int32)
    span_ids = jnp.arange(2, dtype=jnp.int32)
    gain_grad = jnp.zeros((N_SECTION, 2, model_width), jnp.float32)
    for tick_index in range(TICKS):
        fwd_span = jnp.where(phase_ids < tick_index, 1, 0).astype(jnp.int32)
        fwd_rows = fwd_segments[(phase_ids - tick_index) % N_SECTION]
        advanced = lax.map(phase_forward, (forward_blocks, gains, w_query, w_key, w_value, w_out, fwd_span, fwd_rows))
        bwd_span = jnp.where(phase_ids > N_SECTION - 1 - tick_index, 0, 1).astype(jnp.int32)
        bwd_rows = bwd_segments[(phase_ids + tick_index) % N_SECTION]
        returned, gain_terms = lax.map(phase_backward, (stash_blocks[:, tick_index], backward_blocks, gains, w_query, w_key, w_value, w_out, bwd_span, bwd_rows))
        chosen = (span_ids[None, :] == bwd_span[:, None]).astype(jnp.float32)
        gain_grad = gain_grad + chosen[:, :, None] * gain_terms[:, None, :]
        forward_blocks = jnp.roll(advanced, 1, axis=0)
        backward_blocks = jnp.roll(returned, -1, axis=0)
    return (forward_blocks.reshape(N_SECTION, N_DP * R, model_width), backward_blocks.reshape(N_SECTION, N_DP * R, model_width), gain_grad)
```

```python
import functools
import math

import jax
import jax.numpy as jnp
from jax import lax
from jax.experimental import pallas as pl
from jax.experimental.pallas import tpu as pltpu
from jax.sharding import PartitionSpec as P

HD = 128
TICKS = 2
ROPE_BASE = 1000000.0
MESH = pl.DeviceIdType.MESH
F32 = jnp.float32
BF16 = jnp.bfloat16

WIDE = ("in", "out")


def exchange_kernel(kinds, n_dp, n_tensor, *refs):
    count = len(kinds)
    sources, targets = refs[:count], refs[count : 2 * count]
    send_sem, recv_sem, local_sem = refs[2 * count :]
    my_dp, my_tensor = lax.axis_index("dp"), lax.axis_index("tensor")
    wide = any(kind in WIDE for kind in kinds)
    n_all = n_dp * n_tensor
    me = my_dp * n_tensor + my_tensor

    def wide_peer(step):
        peer = lax.rem(me + step, n_all)
        return peer // n_tensor, lax.rem(peer, n_tensor)

    def narrow_peer(step):
        return lax.rem(my_dp + step, n_dp), my_tensor

    barrier = pltpu.get_barrier_semaphore()
    total = n_all if wide else n_dp
    pick = wide_peer if wide else narrow_peer

    @pl.loop(1, total)
    def greet(step):
        peer_dp, peer_tensor = pick(step)
        pl.semaphore_signal(
            barrier, inc=1, device_id={"dp": peer_dp, "tensor": peer_tensor}, device_id_type=MESH
        )

    pl.semaphore_wait(barrier, total - 1)

    def block(job, peer_dp, peer_tensor):
        kind = kinds[job]
        if kind == "ag":
            return sources[job]
        if kind == "out":
            return sources[job].at[peer_dp, peer_tensor]
        return sources[job].at[peer_dp]

    def place(job):
        if kinds[job] in WIDE:
            return targets[job].at[my_dp, my_tensor]
        return targets[job].at[my_dp]

    def remote(job, step):
        peer_dp, peer_tensor = wide_peer(step) if kinds[job] in WIDE else narrow_peer(step)
        return pltpu.make_async_remote_copy(
            src_ref=block(job, peer_dp, peer_tensor),
            dst_ref=place(job),
            send_sem=send_sem.at[job, step],
            recv_sem=recv_sem.at[job, step],
            device_id={"dp": peer_dp, "tensor": peer_tensor},
            device_id_type=MESH,
        )

    def local(job):
        return pltpu.make_async_copy(block(job, my_dp, my_tensor), place(job), local_sem.at[job])

    for job in range(count):

        @pl.loop(1, n_all if kinds[job] in WIDE else n_dp)
        def send(step, job=job):
            remote(job, step).start()

    for job in range(count):
        local(job).start()
    for job in range(count):
        local(job).wait()
    for job in range(count):

        @pl.loop(1, n_all if kinds[job] in WIDE else n_dp)
        def finish(step, job=job):
            remote(job, step).wait()


def exchange(collective_id, *jobs):
    n_dp, n_tensor = lax.axis_size("dp"), lax.axis_size("tensor")
    kinds = tuple(kind for kind, _ in jobs)
    arrays = [value for _, value in jobs]
    shapes = []
    for kind, value in jobs:
        lead = {
            "in": (n_dp, n_tensor) + value.shape[1:],
            "out": value.shape,
            "rs": value.shape,
            "ag": (n_dp,) + value.shape,
        }[kind]
        shapes.append(jax.ShapeDtypeStruct(lead, value.dtype))
    count = len(jobs)
    most = n_dp * n_tensor if any(kind in WIDE for kind in kinds) else n_dp
    return pl.pallas_call(
        functools.partial(exchange_kernel, kinds, n_dp, n_tensor),
        out_shape=shapes,
        in_specs=[pl.BlockSpec(memory_space=pl.ANY)] * count,
        out_specs=[pl.BlockSpec(memory_space=pl.ANY)] * count,
        scratch_shapes=[
            pltpu.SemaphoreType.DMA((count, most)),
            pltpu.SemaphoreType.DMA((count, most)),
            pltpu.SemaphoreType.DMA((count,)),
        ],
        compiler_params=pltpu.CompilerParams(
            collective_id=collective_id, has_side_effects=True
        ),
        name="exchange_" + "_".join(kinds),
    )(*arrays)


def from_behind(value, axis, steps):
    count = lax.axis_size(axis)
    pairs = [(source, (source + steps) % count) for source in range(count)]
    return lax.ppermute(value, axis, pairs)


def rope_tables(segments):
    count_rows = segments.shape[0]
    row_index = jnp.arange(count_rows, dtype=jnp.int32)
    allowed = (segments[:, None] == segments[None, :]) & (row_index[:, None] >= row_index[None, :])
    positions = jnp.sum(allowed.astype(F32), axis=1) - 1.0
    halfway = HD // 2
    frequency = jnp.exp(jnp.arange(halfway, dtype=F32) * (-2.0 * math.log(ROPE_BASE) / HD))
    angles = positions[:, None] * frequency[None, :]
    cosine = jnp.concatenate([jnp.cos(angles), jnp.cos(angles)], axis=1)
    sine_table = jnp.concatenate([jnp.sin(angles), jnp.sin(angles)], axis=1)
    return (cosine[:, None, :], sine_table[:, None, :], allowed)


def rotate(vectors, cosine, sine_table):
    halfway = vectors.shape[-1] // 2
    turned = jnp.concatenate([-vectors[..., halfway:], vectors[..., :halfway]], axis=-1)
    return vectors * cosine + turned * sine_table


def attention(projected, widths, tables):
    cosine, sine_table, allowed = tables
    count_rows = projected.shape[0]
    query_width, key_width = widths
    query_rows = projected[:, :query_width].reshape(count_rows, -1, HD)
    key_rows = projected[:, query_width : query_width + key_width].reshape(count_rows, -1, HD)
    value_rows = projected[:, query_width + key_width :].astype(BF16).reshape(count_rows, -1, HD)
    query_rows = rotate(query_rows, cosine, sine_table).astype(BF16)
    key_rows = rotate(key_rows, cosine, sine_table).astype(BF16)
    key_heads = key_rows.shape[1]
    grouped = query_rows.reshape(count_rows, key_heads, -1, HD)
    scores = jnp.einsum("qkgd,skd->kgqs", grouped.astype(F32), key_rows.astype(F32))
    scores = scores * (1.0 / math.sqrt(HD))
    scores = jnp.where(allowed[None, None], scores, -1e30)
    exponents = jnp.exp(scores)
    soft_weights = (exponents / jnp.sum(exponents, axis=-1, keepdims=True)).astype(BF16)
    mixed_heads = jnp.einsum("kgqs,skd->qkgd", soft_weights.astype(F32), value_rows.astype(F32))
    return mixed_heads.astype(BF16).reshape(count_rows, -1)


def normalise(rows, gain_vector):
    variance = jnp.mean(rows * rows, axis=1, keepdims=True)
    return rows * lax.rsqrt(variance + 1e-06) * gain_vector


def pick_span(table, span):
    return lax.dynamic_index_in_dim(table, span, 0, keepdims=False)


def dot_t(left, right):
    return lax.dot_general(left, right, (((1,), (1,)), ((), ())), preferred_element_type=F32)


def per_device(
    fwd_state, bwd_state, stash, gains, w_query, w_key, w_value, w_out, fwd_segments, bwd_segments
):
    n_dp, n_tensor = lax.axis_size("dp"), lax.axis_size("tensor")
    phase_count = lax.axis_size("section")
    phase_index = lax.axis_index("section")
    own_rows, model_width = fwd_state.shape[1:]
    part = model_width // n_dp
    replica_rows = own_rows * n_tensor
    all_rows = replica_rows * n_dp
    widths = (w_query.shape[3], w_key.shape[3])

    def columns(rows):
        return rows.reshape(own_rows, n_dp, part).transpose(1, 0, 2)

    def project(normed, span):
        normed = normed.reshape(all_rows, part)
        pieces = [
            jnp.dot(normed, pick_span(weight[0], span), preferred_element_type=F32).astype(BF16)
            for weight in (w_query, w_key, w_value)
        ]
        return jnp.concatenate(pieces, axis=1).reshape(n_dp, replica_rows, -1)

    def summed(pieces):
        return jnp.sum(pieces.astype(F32), axis=0)

    def to_owners(term):
        return term.astype(BF16).reshape(n_dp, n_tensor, own_rows, part)

    def rows_of(pieces):
        return jnp.sum(pieces.astype(F32), axis=1).transpose(1, 0, 2).reshape(own_rows, model_width)

    gains32 = gains[0].astype(F32)
    my_part = lax.dynamic_slice_in_dim(gains32, lax.axis_index("dp") * part, part, axis=1)
    stash32 = stash[0].astype(F32)
    fwd_spans = [jnp.where(phase_index < tick, 1, 0).astype(jnp.int32) for tick in range(TICKS)]
    bwd_spans = [
        jnp.where(phase_index > phase_count - 1 - tick, 0, 1).astype(jnp.int32)
        for tick in range(TICKS)
    ]
    fwd_tables = [
        rope_tables(pick_span(fwd_segments[:, 0], (phase_index - tick) % phase_count))
        for tick in range(TICKS)
    ]
    bwd_tables = [
        rope_tables(pick_span(bwd_segments[:, 0], (phase_index + tick) % phase_count))
        for tick in range(TICKS)
    ]

    def forward_in(state_rows, tick):
        gain = pick_span(gains32, fwd_spans[tick])
        return columns(normalise(state_rows.astype(F32), gain).astype(BF16))

    def stash_in(tick):
        gain = pick_span(gains32, bwd_spans[tick])
        return columns(normalise(stash32[tick], gain).astype(BF16))

    def forward_out(mixed, tick):
        mixed = mixed.reshape(all_rows, -1)
        return to_owners(
            jnp.dot(mixed, pick_span(w_out[0], fwd_spans[tick]), preferred_element_type=F32)
        )

    def mixed_gradient(grad, tick):
        grad = grad.reshape(all_rows, part)
        return (
            dot_t(grad, pick_span(w_out[0], bwd_spans[tick]))
            .astype(BF16)
            .reshape(n_dp, replica_rows, -1)
        )

    def attention_gradient(projected, mixed_grad, tick):
        _, pull = jax.vjp(lambda x: attention(x, widths, bwd_tables[tick]), projected)
        return pull(mixed_grad.astype(BF16))[0].astype(BF16)

    def normed_gradient(gradient, normed, tick):
        gradient = gradient.reshape(all_rows, -1)
        span = bwd_spans[tick]
        query_width, key_width = widths
        term = (
            dot_t(gradient[:, :query_width], pick_span(w_query[0], span))
            + dot_t(gradient[:, query_width : query_width + key_width], pick_span(w_key[0], span))
            + dot_t(gradient[:, query_width + key_width :], pick_span(w_value[0], span))
        )
        gain_term = jnp.sum(term * normed.reshape(all_rows, part).astype(F32), axis=0)
        gain_term = gain_term / pick_span(my_part, span)
        gain_term = jnp.broadcast_to(gain_term.reshape(1, -1, 128), (n_dp, part // 128, 128))
        return to_owners(term), gain_term

    def returned_rows(grad_rows, pieces, tick):
        gain = pick_span(gains32, bwd_spans[tick])
        _, pull = jax.vjp(lambda rows: normalise(rows, gain), stash32[tick])
        return (grad_rows.astype(F32) + pull(rows_of(pieces))[0]).astype(BF16)

    span_ids = jnp.arange(2, dtype=jnp.int32)

    def gain_rows(pieces, tick):
        gain = jnp.sum(pieces, axis=1).reshape(model_width)
        chosen = (span_ids == bwd_spans[tick]).astype(F32)
        return chosen[:, None] * gain[None, :]

    state_rows, grad_rows = fwd_state[0], bwd_state[0]
    state, stash0, grad = exchange(
        0, ("in", forward_in(state_rows, 0)), ("in", stash_in(0)), ("in", columns(grad_rows))
    )
    fwd_proj, bwd_proj, mixed_grad, stash1 = exchange(
        1,
        ("rs", project(state, fwd_spans[0])),
        ("rs", project(stash0, bwd_spans[0])),
        ("rs", mixed_gradient(grad, 0)),
        ("in", stash_in(1)),
    )
    mixed = attention(summed(fwd_proj), widths, fwd_tables[0])
    gradient = attention_gradient(summed(bwd_proj), summed(mixed_grad), 0)
    mixed, gradient, bwd_proj = exchange(
        2, ("ag", mixed), ("ag", gradient), ("rs", project(stash1, bwd_spans[1]))
    )
    term, gain_term = normed_gradient(gradient, stash0, 0)
    fwd_pieces, bwd_pieces, gain0 = exchange(
        3, ("out", forward_out(mixed, 0)), ("out", term), ("in", gain_term)
    )
    advanced = (state_rows.astype(F32) + rows_of(fwd_pieces)).astype(BF16)
    state_rows = from_behind(advanced, "section", 1)
    grad_rows = from_behind(returned_rows(grad_rows, bwd_pieces, 0), "section", -1)

    state, grad = exchange(4, ("in", forward_in(state_rows, 1)), ("in", columns(grad_rows)))
    fwd_proj, mixed_grad = exchange(
        5, ("rs", project(state, fwd_spans[1])), ("rs", mixed_gradient(grad, 1))
    )
    mixed = attention(summed(fwd_proj), widths, fwd_tables[1])
    gradient = attention_gradient(summed(bwd_proj), summed(mixed_grad), 1)
    mixed, gradient = exchange(6, ("ag", mixed), ("ag", gradient))
    term, gain_term = normed_gradient(gradient, stash1, 1)
    fwd_pieces, bwd_pieces, gain1 = exchange(
        7, ("out", forward_out(mixed, 1)), ("out", term), ("in", gain_term)
    )
    advanced = (state_rows.astype(F32) + rows_of(fwd_pieces)).astype(BF16)
    state_rows = from_behind(advanced, "section", 1)
    grad_rows = from_behind(returned_rows(grad_rows, bwd_pieces, 1), "section", -1)
    gain_total = gain_rows(gain0, 0) + gain_rows(gain1, 1)
    return (state_rows[None], grad_rows[None], gain_total[None])


def solution(mesh):
    in_specs = (
        P("section", ("dp", "tensor"), None),
        P("section", ("dp", "tensor"), None),
        P("section", None, ("dp", "tensor"), None),
        P("section", None, None),
        P("section", None, "dp", "tensor"),
        P("section", None, "dp", "tensor"),
        P("section", None, "dp", "tensor"),
        P("section", None, "tensor", "dp"),
        P(None, "dp", None),
        P(None, "dp", None),
    )
    out_specs = (
        P("section", ("dp", "tensor"), None),
        P("section", ("dp", "tensor"), None),
        P("section", None, None),
    )
    return jax.shard_map(
        per_device, mesh=mesh, in_specs=in_specs, out_specs=out_specs, check_vma=False
    )
```

```python
import functools
import math

import jax
import jax.numpy as jnp
from jax import lax
from jax.experimental import pallas as pl
from jax.experimental.pallas import tpu as pltpu
from jax.sharding import PartitionSpec as P

HD = 128
TICKS = 2
ROPE_BASE = 1000000.0
MESH = pl.DeviceIdType.MESH
F32 = jnp.float32
BF16 = jnp.bfloat16

WIDE = ("out", "all")


def exchange_kernel(kinds, n_dp, n_tensor, *refs):
    count = len(kinds)
    sources, targets = refs[:count], refs[count : 2 * count]
    send_sem, recv_sem, up_sem, down_sem, local_sem = refs[2 * count :]
    my_dp, my_tensor = lax.axis_index("dp"), lax.axis_index("tensor")
    n_all = n_dp * n_tensor
    me = my_dp * n_tensor + my_tensor
    order = sorted(range(count), key=lambda job: ("in", "out", "all", "rs", "ag").index(kinds[job]))
    flowing = [job for job in order if kinds[job] == "in"]

    def wide_peer(step):
        peer = lax.rem(me + step, n_all)
        return peer // n_tensor, lax.rem(peer, n_tensor)

    def narrow_peer(step):
        return lax.rem(my_dp + step, n_dp), my_tensor

    barrier = pltpu.get_barrier_semaphore()
    wide = any(kind in WIDE + ("in",) for kind in kinds)
    total = n_all if wide else n_dp
    pick = wide_peer if wide else narrow_peer

    @pl.loop(1, total)
    def greet(step):
        peer_dp, peer_tensor = pick(step)
        pl.semaphore_signal(
            barrier, inc=1, device_id={"dp": peer_dp, "tensor": peer_tensor}, device_id_type=MESH
        )

    pl.semaphore_wait(barrier, total - 1)

    def block(job, peer_dp, peer_tensor):
        kind = kinds[job]
        if kind in ("ag", "all"):
            return sources[job]
        if kind == "out":
            return sources[job].at[peer_dp, peer_tensor]
        return sources[job].at[peer_dp]

    def place(job):
        if kinds[job] in WIDE + ("in",):
            return targets[job].at[my_dp, my_tensor]
        return targets[job].at[my_dp]

    def steps(job):
        return n_all if kinds[job] in WIDE else n_dp

    def remote(job, step):
        peer_dp, peer_tensor = wide_peer(step) if kinds[job] in WIDE else narrow_peer(step)
        return pltpu.make_async_remote_copy(
            src_ref=block(job, peer_dp, peer_tensor),
            dst_ref=place(job),
            send_sem=send_sem.at[job, step],
            recv_sem=recv_sem.at[job, step],
            device_id={"dp": peer_dp, "tensor": peer_tensor},
            device_id_type=MESH,
        )

    def local(job):
        return pltpu.make_async_copy(block(job, my_dp, my_tensor), place(job), local_sem.at[job])

    def hop(job, step, source, move):
        owner = lax.rem(my_dp + n_dp - step, n_dp)
        sems = up_sem if move == 1 else down_sem
        return pltpu.make_async_remote_copy(
            src_ref=targets[job].at[owner, source],
            dst_ref=targets[job].at[owner, source],
            send_sem=sems.at[0, job, step, source],
            recv_sem=sems.at[1, job, step, source],
            device_id={"dp": my_dp, "tensor": lax.rem(my_tensor + move + n_tensor, n_tensor)},
            device_id_type=MESH,
        )

    for job in order:

        @pl.loop(1, steps(job))
        def send(step, job=job):
            remote(job, step).start()

    for job in order:
        local(job).start()
    for job in order:
        local(job).wait()

    def pass_on(job, step, source):
        @pl.when((source <= my_tensor) & (my_tensor < n_tensor - 1))
        def up():
            hop(job, step, source, 1).start()

        @pl.when((source >= my_tensor) & (my_tensor > 0))
        def down():
            hop(job, step, source, -1).start()

    for job in flowing:
        pass_on(job, 0, my_tensor)

        @pl.loop(1, n_dp)
        def first(step, job=job):
            remote(job, step).wait_recv()
            pass_on(job, step, my_tensor)

    for job in flowing:

        @pl.loop(1, n_tensor)
        def onward(distance, job=job):
            below, above = my_tensor - distance, my_tensor + distance

            @pl.loop(0, n_dp)
            def piece(step):
                @pl.when(below >= 0)
                def from_below():
                    hop(job, step, below, 1).wait_recv()
                    pass_on(job, step, below)

                @pl.when(above < n_tensor)
                def from_above():
                    hop(job, step, above, -1).wait_recv()
                    pass_on(job, step, above)

    for job in flowing:

        @pl.loop(1, n_dp)
        def sent(step, job=job):
            remote(job, step).wait_send()

        @pl.loop(0, n_tensor)
        def handed(source, job=job):
            @pl.loop(0, n_dp)
            def piece(step):
                @pl.when((source <= my_tensor) & (my_tensor < n_tensor - 1))
                def up():
                    hop(job, step, source, 1).wait_send()

                @pl.when((source >= my_tensor) & (my_tensor > 0))
                def down():
                    hop(job, step, source, -1).wait_send()

    for job in order:
        if job not in flowing:

            @pl.loop(1, steps(job))
            def finish(step, job=job):
                remote(job, step).wait()


def exchange(collective_id, *jobs):
    n_dp, n_tensor = lax.axis_size("dp"), lax.axis_size("tensor")
    kinds = tuple(kind for kind, _ in jobs)
    arrays = [value for _, value in jobs]
    shapes = []
    for kind, value in jobs:
        lead = {
            "in": (n_dp, n_tensor) + value.shape[1:],
            "out": value.shape,
            "all": (n_dp, n_tensor) + value.shape,
            "rs": value.shape,
            "ag": (n_dp,) + value.shape,
        }[kind]
        shapes.append(jax.ShapeDtypeStruct(lead, value.dtype))
    count = len(jobs)
    most = n_dp * n_tensor
    return pl.pallas_call(
        functools.partial(exchange_kernel, kinds, n_dp, n_tensor),
        out_shape=shapes,
        in_specs=[pl.BlockSpec(memory_space=pl.ANY)] * count,
        out_specs=[pl.BlockSpec(memory_space=pl.ANY)] * count,
        scratch_shapes=[
            pltpu.SemaphoreType.DMA((count, most)),
            pltpu.SemaphoreType.DMA((count, most)),
            pltpu.SemaphoreType.DMA((2, count, n_dp, n_tensor)),
            pltpu.SemaphoreType.DMA((2, count, n_dp, n_tensor)),
            pltpu.SemaphoreType.DMA((count,)),
        ],
        compiler_params=pltpu.CompilerParams(
            collective_id=collective_id, has_side_effects=True
        ),
        name="exchange_" + "_".join(kinds),
    )(*arrays)


def from_behind(value, axis, steps):
    count = lax.axis_size(axis)
    pairs = [(source, (source + steps) % count) for source in range(count)]
    return lax.ppermute(value, axis, pairs)


def rope_tables(segments):
    count_rows = segments.shape[0]
    row_index = jnp.arange(count_rows, dtype=jnp.int32)
    allowed = (segments[:, None] == segments[None, :]) & (row_index[:, None] >= row_index[None, :])
    positions = jnp.sum(allowed.astype(F32), axis=1) - 1.0
    halfway = HD // 2
    frequency = jnp.exp(jnp.arange(halfway, dtype=F32) * (-2.0 * math.log(ROPE_BASE) / HD))
    angles = positions[:, None] * frequency[None, :]
    cosine = jnp.concatenate([jnp.cos(angles), jnp.cos(angles)], axis=1)
    sine_table = jnp.concatenate([jnp.sin(angles), jnp.sin(angles)], axis=1)
    return (cosine[:, None, :], sine_table[:, None, :], allowed)


def rotate(vectors, cosine, sine_table):
    halfway = vectors.shape[-1] // 2
    turned = jnp.concatenate([-vectors[..., halfway:], vectors[..., :halfway]], axis=-1)
    return vectors * cosine + turned * sine_table


def attention(projected, widths, tables):
    cosine, sine_table, allowed = tables
    count_rows = projected.shape[0]
    query_width, key_width = widths
    query_rows = projected[:, :query_width].reshape(count_rows, -1, HD)
    key_rows = projected[:, query_width : query_width + key_width].reshape(count_rows, -1, HD)
    value_rows = projected[:, query_width + key_width :].astype(BF16).reshape(count_rows, -1, HD)
    query_rows = rotate(query_rows, cosine, sine_table).astype(BF16)
    key_rows = rotate(key_rows, cosine, sine_table).astype(BF16)
    key_heads = key_rows.shape[1]
    grouped = query_rows.reshape(count_rows, key_heads, -1, HD)
    scores = jnp.einsum("qkgd,skd->kgqs", grouped.astype(F32), key_rows.astype(F32))
    scores = scores * (1.0 / math.sqrt(HD))
    scores = jnp.where(allowed[None, None], scores, -1e30)
    exponents = jnp.exp(scores)
    soft_weights = (exponents / jnp.sum(exponents, axis=-1, keepdims=True)).astype(BF16)
    mixed_heads = jnp.einsum("kgqs,skd->qkgd", soft_weights.astype(F32), value_rows.astype(F32))
    return mixed_heads.astype(BF16).reshape(count_rows, -1)


def normalise(rows, gain_vector):
    variance = jnp.mean(rows * rows, axis=1, keepdims=True)
    return rows * lax.rsqrt(variance + 1e-06) * gain_vector


def pick_span(table, span):
    return lax.dynamic_index_in_dim(table, span, 0, keepdims=False)


def dot_t(left, right):
    return lax.dot_general(left, right, (((1,), (1,)), ((), ())), preferred_element_type=F32)


def per_device(
    fwd_state, bwd_state, stash, gains, w_query, w_key, w_value, w_out, fwd_segments, bwd_segments
):
    n_dp, n_tensor = lax.axis_size("dp"), lax.axis_size("tensor")
    phase_count = lax.axis_size("section")
    phase_index = lax.axis_index("section")
    own_rows, model_width = fwd_state.shape[1:]
    part = model_width // n_dp
    replica_rows = own_rows * n_tensor
    all_rows = replica_rows * n_dp
    widths = (w_query.shape[3], w_key.shape[3])

    def columns(rows):
        return rows.reshape(own_rows, n_dp, part).transpose(1, 0, 2)

    def project(normed, span):
        normed = normed.reshape(all_rows, part)
        pieces = [
            jnp.dot(normed, pick_span(weight[0], span), preferred_element_type=F32).astype(BF16)
            for weight in (w_query, w_key, w_value)
        ]
        return jnp.concatenate(pieces, axis=1).reshape(n_dp, replica_rows, -1)

    def summed(pieces):
        return jnp.sum(pieces.astype(F32), axis=0)

    def to_owners(term):
        return term.astype(BF16).reshape(n_dp, n_tensor, own_rows, part)

    def rows_of(pieces):
        return jnp.sum(pieces.astype(F32), axis=1).transpose(1, 0, 2).reshape(own_rows, model_width)

    gains32 = gains[0].astype(F32)
    my_part = lax.dynamic_slice_in_dim(gains32, lax.axis_index("dp") * part, part, axis=1)
    stash32 = stash[0].astype(F32)
    fwd_spans = [jnp.where(phase_index < tick, 1, 0).astype(jnp.int32) for tick in range(TICKS)]
    bwd_spans = [
        jnp.where(phase_index > phase_count - 1 - tick, 0, 1).astype(jnp.int32)
        for tick in range(TICKS)
    ]
    fwd_tables = [
        rope_tables(pick_span(fwd_segments[:, 0], (phase_index - tick) % phase_count))
        for tick in range(TICKS)
    ]
    bwd_tables = [
        rope_tables(pick_span(bwd_segments[:, 0], (phase_index + tick) % phase_count))
        for tick in range(TICKS)
    ]

    def forward_in(state_rows, tick):
        gain = pick_span(gains32, fwd_spans[tick])
        return columns(normalise(state_rows.astype(F32), gain).astype(BF16))

    def stash_in(tick):
        gain = pick_span(gains32, bwd_spans[tick])
        return columns(normalise(stash32[tick], gain).astype(BF16))

    def forward_out(mixed, tick):
        mixed = mixed.reshape(all_rows, -1)
        return to_owners(
            jnp.dot(mixed, pick_span(w_out[0], fwd_spans[tick]), preferred_element_type=F32)
        )

    def mixed_gradient(grad, tick):
        grad = grad.reshape(all_rows, part)
        return (
            dot_t(grad, pick_span(w_out[0], bwd_spans[tick]))
            .astype(BF16)
            .reshape(n_dp, replica_rows, -1)
        )

    def attention_gradient(projected, mixed_grad, tick):
        _, pull = jax.vjp(lambda x: attention(x, widths, bwd_tables[tick]), projected)
        return pull(mixed_grad.astype(BF16))[0].astype(BF16)

    def normed_gradient(gradient, normed, tick):
        gradient = gradient.reshape(all_rows, -1)
        span = bwd_spans[tick]
        query_width, key_width = widths
        term = (
            dot_t(gradient[:, :query_width], pick_span(w_query[0], span))
            + dot_t(gradient[:, query_width : query_width + key_width], pick_span(w_key[0], span))
            + dot_t(gradient[:, query_width + key_width :], pick_span(w_value[0], span))
        )
        gain_term = jnp.sum(term * normed.reshape(all_rows, part).astype(F32), axis=0)
        gain_term = gain_term / pick_span(my_part, span)
        return to_owners(term), gain_term.reshape(-1, 128)

    def returned_rows(grad_rows, pieces, tick):
        gain = pick_span(gains32, bwd_spans[tick])
        _, pull = jax.vjp(lambda rows: normalise(rows, gain), stash32[tick])
        return (grad_rows.astype(F32) + pull(rows_of(pieces))[0]).astype(BF16)

    span_ids = jnp.arange(2, dtype=jnp.int32)

    def gain_rows(pieces, tick):
        gain = jnp.sum(pieces, axis=1).reshape(model_width)
        chosen = (span_ids == bwd_spans[tick]).astype(F32)
        return chosen[:, None] * gain[None, :]

    state_rows, grad_rows = fwd_state[0], bwd_state[0]
    (stash0,) = exchange(0, ("in", stash_in(0)))
    grad, bwd_proj = exchange(
        1, ("in", columns(grad_rows)), ("rs", project(stash0, bwd_spans[0]))
    )
    state, mixed_grad = exchange(
        2, ("in", forward_in(state_rows, 0)), ("rs", mixed_gradient(grad, 0))
    )
    gradient = attention_gradient(summed(bwd_proj), summed(mixed_grad), 0)
    stash1, fwd_proj, gradient = exchange(
        3, ("in", stash_in(1)), ("rs", project(state, fwd_spans[0])), ("ag", gradient)
    )
    term, gain_term = normed_gradient(gradient, stash0, 0)
    mixed = attention(summed(fwd_proj), widths, fwd_tables[0])
    bwd_pieces, gain0, mixed = exchange(4, ("out", term), ("all", gain_term), ("ag", mixed))
    grad_rows = from_behind(returned_rows(grad_rows, bwd_pieces, 0), "section", -1)
    fwd_pieces, grad, bwd_proj = exchange(
        5,
        ("out", forward_out(mixed, 0)),
        ("in", columns(grad_rows)),
        ("rs", project(stash1, bwd_spans[1])),
    )
    advanced = (state_rows.astype(F32) + rows_of(fwd_pieces)).astype(BF16)
    state_rows = from_behind(advanced, "section", 1)
    state, mixed_grad = exchange(
        6, ("in", forward_in(state_rows, 1)), ("rs", mixed_gradient(grad, 1))
    )
    gradient = attention_gradient(summed(bwd_proj), summed(mixed_grad), 1)
    fwd_proj, gradient = exchange(
        7, ("rs", project(state, fwd_spans[1])), ("ag", gradient)
    )
    term, gain_term = normed_gradient(gradient, stash1, 1)
    mixed = attention(summed(fwd_proj), widths, fwd_tables[1])
    bwd_pieces, gain1, mixed = exchange(8, ("out", term), ("all", gain_term), ("ag", mixed))
    grad_rows = from_behind(returned_rows(grad_rows, bwd_pieces, 1), "section", -1)
    (fwd_pieces,) = exchange(9, ("out", forward_out(mixed, 1)))
    advanced = (state_rows.astype(F32) + rows_of(fwd_pieces)).astype(BF16)
    state_rows = from_behind(advanced, "section", 1)
    gain_total = gain_rows(gain0, 0) + gain_rows(gain1, 1)
    return (state_rows[None], grad_rows[None], gain_total[None])


def solution(mesh):
    in_specs = (
        P("section", ("dp", "tensor"), None),
        P("section", ("dp", "tensor"), None),
        P("section", None, ("dp", "tensor"), None),
        P("section", None, None),
        P("section", None, "dp", "tensor"),
        P("section", None, "dp", "tensor"),
        P("section", None, "dp", "tensor"),
        P("section", None, "tensor", "dp"),
        P(None, "dp", None),
        P(None, "dp", None),
    )
    out_specs = (
        P("section", ("dp", "tensor"), None),
        P("section", ("dp", "tensor"), None),
        P("section", None, None),
    )
    return jax.shard_map(
        per_device, mesh=mesh, in_specs=in_specs, out_specs=out_specs, check_vma=False
    )
```

```python
import functools
import math

import jax
import jax.numpy as jnp
from jax import lax
from jax.experimental import pallas as pl
from jax.experimental.pallas import tpu as pltpu
from jax.sharding import PartitionSpec as P

HD = 128
TICKS = 2
ROPE_BASE = 1000000.0
MESH = pl.DeviceIdType.MESH
F32 = jnp.float32
BF16 = jnp.bfloat16

WIDE = ("out", "all")


def exchange_kernel(kinds, n_dp, n_tensor, *refs):
    count = len(kinds)
    sources, targets = refs[:count], refs[count : 2 * count]
    send_sem, recv_sem, up_sem, down_sem, local_sem = refs[2 * count :]
    my_dp, my_tensor = lax.axis_index("dp"), lax.axis_index("tensor")
    n_all = n_dp * n_tensor
    me = my_dp * n_tensor + my_tensor
    order = sorted(range(count), key=lambda job: ("in", "out", "all", "rs", "ag").index(kinds[job]))
    flowing = [job for job in order if kinds[job] == "in"]

    def wide_peer(step):
        peer = lax.rem(me + step, n_all)
        return peer // n_tensor, lax.rem(peer, n_tensor)

    def narrow_peer(step):
        return lax.rem(my_dp + step, n_dp), my_tensor

    barrier = pltpu.get_barrier_semaphore()
    wide = any(kind in WIDE + ("in",) for kind in kinds)
    total = n_all if wide else n_dp
    pick = wide_peer if wide else narrow_peer

    @pl.loop(1, total)
    def greet(step):
        peer_dp, peer_tensor = pick(step)
        pl.semaphore_signal(
            barrier, inc=1, device_id={"dp": peer_dp, "tensor": peer_tensor}, device_id_type=MESH
        )

    pl.semaphore_wait(barrier, total - 1)

    def block(job, peer_dp, peer_tensor):
        kind = kinds[job]
        if kind in ("ag", "all"):
            return sources[job]
        if kind == "out":
            return sources[job].at[peer_dp, peer_tensor]
        return sources[job].at[peer_dp]

    def place(job):
        if kinds[job] in WIDE + ("in",):
            return targets[job].at[my_dp, my_tensor]
        return targets[job].at[my_dp]

    def steps(job):
        return n_all if kinds[job] in WIDE else n_dp

    def remote(job, step):
        peer_dp, peer_tensor = wide_peer(step) if kinds[job] in WIDE else narrow_peer(step)
        return pltpu.make_async_remote_copy(
            src_ref=block(job, peer_dp, peer_tensor),
            dst_ref=place(job),
            send_sem=send_sem.at[job, step],
            recv_sem=recv_sem.at[job, step],
            device_id={"dp": peer_dp, "tensor": peer_tensor},
            device_id_type=MESH,
        )

    def local(job):
        return pltpu.make_async_copy(block(job, my_dp, my_tensor), place(job), local_sem.at[job])

    def hop(job, step, source, move):
        owner = lax.rem(my_dp + n_dp - step, n_dp)
        sems = up_sem if move == 1 else down_sem
        return pltpu.make_async_remote_copy(
            src_ref=targets[job].at[owner, source],
            dst_ref=targets[job].at[owner, source],
            send_sem=sems.at[0, job, step, source],
            recv_sem=sems.at[1, job, step, source],
            device_id={"dp": my_dp, "tensor": lax.rem(my_tensor + move + n_tensor, n_tensor)},
            device_id_type=MESH,
        )

    for job in order:

        @pl.loop(1, steps(job))
        def send(step, job=job):
            remote(job, step).start()

    for job in order:
        local(job).start()
    for job in order:
        local(job).wait()

    def pass_on(job, step, source):
        @pl.when((source <= my_tensor) & (my_tensor < n_tensor - 1))
        def up():
            hop(job, step, source, 1).start()

        @pl.when((source >= my_tensor) & (my_tensor > 0))
        def down():
            hop(job, step, source, -1).start()

    for job in flowing:
        pass_on(job, 0, my_tensor)

        @pl.loop(1, n_dp)
        def first(step, job=job):
            remote(job, step).wait_recv()
            pass_on(job, step, my_tensor)

    for job in flowing:

        @pl.loop(1, n_tensor)
        def onward(distance, job=job):
            below, above = my_tensor - distance, my_tensor + distance

            @pl.loop(0, n_dp)
            def piece(step):
                @pl.when(below >= 0)
                def from_below():
                    hop(job, step, below, 1).wait_recv()
                    pass_on(job, step, below)

                @pl.when(above < n_tensor)
                def from_above():
                    hop(job, step, above, -1).wait_recv()
                    pass_on(job, step, above)

    for job in flowing:

        @pl.loop(1, n_dp)
        def sent(step, job=job):
            remote(job, step).wait_send()

        @pl.loop(0, n_tensor)
        def handed(source, job=job):
            @pl.loop(0, n_dp)
            def piece(step):
                @pl.when((source <= my_tensor) & (my_tensor < n_tensor - 1))
                def up():
                    hop(job, step, source, 1).wait_send()

                @pl.when((source >= my_tensor) & (my_tensor > 0))
                def down():
                    hop(job, step, source, -1).wait_send()

    for job in order:
        if job not in flowing:

            @pl.loop(1, steps(job))
            def finish(step, job=job):
                remote(job, step).wait()


def exchange(collective_id, *jobs):
    n_dp, n_tensor = lax.axis_size("dp"), lax.axis_size("tensor")
    kinds = tuple(kind for kind, _ in jobs)
    arrays = [value for _, value in jobs]
    shapes = []
    for kind, value in jobs:
        lead = {
            "in": (n_dp, n_tensor) + value.shape[1:],
            "out": value.shape,
            "all": (n_dp, n_tensor) + value.shape,
            "rs": value.shape,
            "ag": (n_dp,) + value.shape,
        }[kind]
        shapes.append(jax.ShapeDtypeStruct(lead, value.dtype))
    count = len(jobs)
    most = n_dp * n_tensor
    return pl.pallas_call(
        functools.partial(exchange_kernel, kinds, n_dp, n_tensor),
        out_shape=shapes,
        in_specs=[pl.BlockSpec(memory_space=pl.ANY)] * count,
        out_specs=[pl.BlockSpec(memory_space=pl.ANY)] * count,
        scratch_shapes=[
            pltpu.SemaphoreType.DMA((count, most)),
            pltpu.SemaphoreType.DMA((count, most)),
            pltpu.SemaphoreType.DMA((2, count, n_dp, n_tensor)),
            pltpu.SemaphoreType.DMA((2, count, n_dp, n_tensor)),
            pltpu.SemaphoreType.DMA((count,)),
        ],
        compiler_params=pltpu.CompilerParams(
            collective_id=collective_id, has_side_effects=True
        ),
        name="exchange_" + "_".join(kinds),
    )(*arrays)


def from_behind(value, axis, steps):
    count = lax.axis_size(axis)
    pairs = [(source, (source + steps) % count) for source in range(count)]
    return lax.ppermute(value, axis, pairs)


def rope_tables(segments):
    count_rows = segments.shape[1]
    row_index = jnp.arange(count_rows, dtype=jnp.int32)
    allowed = (segments[:, :, None] == segments[:, None, :]) & (
        row_index[:, None] >= row_index[None, :]
    )[None]
    allowed = allowed.astype(F32)
    positions = jnp.sum(allowed, axis=2) - 1.0
    halfway = HD // 2
    frequency = jnp.exp(jnp.arange(halfway, dtype=F32) * (-2.0 * math.log(ROPE_BASE) / HD))
    angles = positions[:, :, None] * frequency
    cosine, sine = jnp.cos(angles), jnp.sin(angles)
    return (
        jnp.concatenate([cosine, cosine], axis=2),
        jnp.concatenate([-sine, sine], axis=2),
        allowed,
    )


def dot(left, right, contract):
    return lax.dot_general(left, right, (contract, ((), ())), preferred_element_type=F32)


ROWS_COLUMNS, COLUMNS_COLUMNS, ROWS_ROWS = ((1,), (0,)), ((1,), (1,)), ((0,), (0,))


def total(pieces, first):
    value = pieces[0, :, first : first + HD].astype(F32)
    for index in range(1, pieces.shape[0]):
        value = value + pieces[index, :, first : first + HD].astype(F32)
    return value


def turn(value, cosine, sine):
    return value * cosine + pltpu.roll(value, HD // 2, 1) * sine


def softmax(query, key, allowed):
    scores = dot(query, key, COLUMNS_COLUMNS) * (1.0 / math.sqrt(HD))
    exponents = jnp.exp(jnp.where(allowed > 0.5, scores, -1e30))
    return exponents / jnp.sum(exponents, axis=1, keepdims=True)


def attention_kernel(widths, pieces, cosine, sine, allowed, mixed):
    query_width, key_width = widths
    group = query_width // key_width
    cos, sin, keep = cosine[...], sine[...], allowed[...]
    for key_head in range(key_width // HD):
        key = turn(total(pieces, query_width + key_head * HD), cos, sin).astype(BF16)
        value = total(pieces, query_width + key_width + key_head * HD).astype(BF16)
        for head in range(key_head * group, (key_head + 1) * group):
            query = turn(total(pieces, head * HD), cos, sin).astype(BF16)
            probs = softmax(query, key, keep).astype(BF16)
            mixed[:, head * HD : (head + 1) * HD] = dot(probs, value, ROWS_COLUMNS).astype(BF16)


def attention_gradient_kernel(widths, pieces, grads, cosine, sine, allowed, gradient):
    query_width, key_width = widths
    group = query_width // key_width
    cos, sin, keep = cosine[...], sine[...], allowed[...]
    for key_head in range(key_width // HD):
        key_at = query_width + key_head * HD
        value_at = key_at + key_width
        key = turn(total(pieces, key_at), cos, sin).astype(BF16)
        value = total(pieces, value_at).astype(BF16)
        key_grad = jnp.zeros(key.shape, F32)
        value_grad = jnp.zeros(key.shape, F32)
        for head in range(key_head * group, (key_head + 1) * group):
            query = turn(total(pieces, head * HD), cos, sin).astype(BF16)
            mixed_grad = total(grads, head * HD).astype(BF16)
            probs = softmax(query, key, keep)
            value_grad = value_grad + dot(probs.astype(BF16), mixed_grad, ROWS_ROWS)
            probs_grad = dot(mixed_grad, value, COLUMNS_COLUMNS).astype(BF16).astype(F32)
            mean = jnp.sum(probs_grad * probs, axis=1, keepdims=True)
            scores_grad = (probs * (probs_grad - mean) * (1.0 / math.sqrt(HD))).astype(BF16)
            query_grad = dot(scores_grad, key, ROWS_COLUMNS).astype(BF16).astype(F32)
            gradient[:, head * HD : (head + 1) * HD] = turn(query_grad, cos, -sin).astype(BF16)
            key_grad = key_grad + dot(scores_grad, query, ROWS_ROWS)
        key_grad = key_grad.astype(BF16).astype(F32)
        gradient[:, key_at : key_at + HD] = turn(key_grad, cos, -sin).astype(BF16)
        gradient[:, value_at : value_at + HD] = value_grad.astype(BF16)


def in_vmem(kernel, widths, out_width, *operands):
    count_rows = operands[0].shape[1]
    return pl.pallas_call(
        functools.partial(kernel, widths),
        out_shape=jax.ShapeDtypeStruct((count_rows, out_width), BF16),
        in_specs=[pl.BlockSpec(memory_space=pltpu.VMEM)] * len(operands),
        out_specs=pl.BlockSpec(memory_space=pltpu.VMEM),
        compiler_params=pltpu.CompilerParams(vmem_limit_bytes=32 * 1024 * 1024),
    )(*operands)


def normalise(rows, gain_vector):
    variance = jnp.mean(rows * rows, axis=1, keepdims=True)
    return rows * lax.rsqrt(variance + 1e-06) * gain_vector


def pick_span(table, span):
    return lax.dynamic_index_in_dim(table, span, 0, keepdims=False)


def dot_t(left, right):
    return lax.dot_general(left, right, (((1,), (1,)), ((), ())), preferred_element_type=F32)


def per_device(
    fwd_state, bwd_state, stash, gains, w_query, w_key, w_value, w_out, fwd_segments, bwd_segments
):
    n_dp, n_tensor = lax.axis_size("dp"), lax.axis_size("tensor")
    phase_count = lax.axis_size("section")
    phase_index = lax.axis_index("section")
    own_rows, model_width = fwd_state.shape[1:]
    part = model_width // n_dp
    replica_rows = own_rows * n_tensor
    all_rows = replica_rows * n_dp
    widths = (w_query.shape[3], w_key.shape[3])

    def columns(rows):
        return rows.reshape(own_rows, n_dp, part).transpose(1, 0, 2)

    def project(normed, span):
        normed = normed.reshape(all_rows, part)
        pieces = [
            jnp.dot(normed, pick_span(weight[0], span), preferred_element_type=F32).astype(BF16)
            for weight in (w_query, w_key, w_value)
        ]
        return jnp.concatenate(pieces, axis=1).reshape(n_dp, replica_rows, -1)

    def to_owners(term):
        return term.astype(BF16).reshape(n_dp, n_tensor, own_rows, part)

    def rows_of(pieces):
        return jnp.sum(pieces.astype(F32), axis=1).transpose(1, 0, 2).reshape(own_rows, model_width)

    gains32 = gains[0].astype(F32)
    my_part = lax.dynamic_slice_in_dim(gains32, lax.axis_index("dp") * part, part, axis=1)
    stash32 = stash[0].astype(F32)
    fwd_spans = [jnp.where(phase_index < tick, 1, 0).astype(jnp.int32) for tick in range(TICKS)]
    bwd_spans = [
        jnp.where(phase_index > phase_count - 1 - tick, 0, 1).astype(jnp.int32)
        for tick in range(TICKS)
    ]
    rows_ids = [
        pick_span(fwd_segments[:, 0], (phase_index - tick) % phase_count) for tick in range(TICKS)
    ] + [pick_span(bwd_segments[:, 0], (phase_index + tick) % phase_count) for tick in range(TICKS)]
    tables = rope_tables(jnp.stack(rows_ids))

    def attention(projected, tick):
        return in_vmem(
            attention_kernel, widths, widths[0], projected, *[table[tick] for table in tables]
        )

    def forward_in(state_rows, tick):
        gain = pick_span(gains32, fwd_spans[tick])
        return columns(normalise(state_rows.astype(F32), gain).astype(BF16))

    def stash_in(tick):
        gain = pick_span(gains32, bwd_spans[tick])
        return columns(normalise(stash32[tick], gain).astype(BF16))

    def forward_out(mixed, tick):
        mixed = mixed.reshape(all_rows, -1)
        return to_owners(
            jnp.dot(mixed, pick_span(w_out[0], fwd_spans[tick]), preferred_element_type=F32)
        )

    def mixed_gradient(grad, tick):
        grad = grad.reshape(all_rows, part)
        return (
            dot_t(grad, pick_span(w_out[0], bwd_spans[tick]))
            .astype(BF16)
            .reshape(n_dp, replica_rows, -1)
        )

    def attention_gradient(projected, mixed_grad, tick):
        return in_vmem(
            attention_gradient_kernel,
            widths,
            widths[0] + 2 * widths[1],
            projected,
            mixed_grad,
            *[table[TICKS + tick] for table in tables],
        )

    def normed_gradient(gradient, normed, tick):
        gradient = gradient.reshape(all_rows, -1)
        span = bwd_spans[tick]
        query_width, key_width = widths
        term = (
            dot_t(gradient[:, :query_width], pick_span(w_query[0], span))
            + dot_t(gradient[:, query_width : query_width + key_width], pick_span(w_key[0], span))
            + dot_t(gradient[:, query_width + key_width :], pick_span(w_value[0], span))
        )
        gain_term = jnp.sum(term * normed.reshape(all_rows, part).astype(F32), axis=0)
        gain_term = gain_term / pick_span(my_part, span)
        return to_owners(term), gain_term.reshape(-1, 128)

    def returned_rows(grad_rows, pieces, tick):
        gain = pick_span(gains32, bwd_spans[tick])
        _, pull = jax.vjp(lambda rows: normalise(rows, gain), stash32[tick])
        return (grad_rows.astype(F32) + pull(rows_of(pieces))[0]).astype(BF16)

    span_ids = jnp.arange(2, dtype=jnp.int32)

    def gain_rows(pieces, tick):
        gain = jnp.sum(pieces, axis=1).reshape(model_width)
        chosen = (span_ids == bwd_spans[tick]).astype(F32)
        return chosen[:, None] * gain[None, :]

    state_rows, grad_rows = fwd_state[0], bwd_state[0]
    (stash0,) = exchange(0, ("in", stash_in(0)))
    grad, bwd_proj = exchange(
        1, ("in", columns(grad_rows)), ("rs", project(stash0, bwd_spans[0]))
    )
    state, mixed_grad = exchange(
        2, ("in", forward_in(state_rows, 0)), ("rs", mixed_gradient(grad, 0))
    )
    gradient = attention_gradient(bwd_proj, mixed_grad, 0)
    stash1, fwd_proj, gradient = exchange(
        3, ("in", stash_in(1)), ("rs", project(state, fwd_spans[0])), ("ag", gradient)
    )
    term, gain_term = normed_gradient(gradient, stash0, 0)
    mixed = attention(fwd_proj, 0)
    bwd_pieces, gain0, mixed = exchange(4, ("out", term), ("all", gain_term), ("ag", mixed))
    grad_rows = from_behind(returned_rows(grad_rows, bwd_pieces, 0), "section", -1)
    fwd_pieces, grad, bwd_proj = exchange(
        5,
        ("out", forward_out(mixed, 0)),
        ("in", columns(grad_rows)),
        ("rs", project(stash1, bwd_spans[1])),
    )
    advanced = (state_rows.astype(F32) + rows_of(fwd_pieces)).astype(BF16)
    state_rows = from_behind(advanced, "section", 1)
    state, mixed_grad = exchange(
        6, ("in", forward_in(state_rows, 1)), ("rs", mixed_gradient(grad, 1))
    )
    gradient = attention_gradient(bwd_proj, mixed_grad, 1)
    fwd_proj, gradient = exchange(
        7, ("rs", project(state, fwd_spans[1])), ("ag", gradient)
    )
    term, gain_term = normed_gradient(gradient, stash1, 1)
    mixed = attention(fwd_proj, 1)
    bwd_pieces, gain1, mixed = exchange(8, ("out", term), ("all", gain_term), ("ag", mixed))
    grad_rows = from_behind(returned_rows(grad_rows, bwd_pieces, 1), "section", -1)
    (fwd_pieces,) = exchange(9, ("out", forward_out(mixed, 1)))
    advanced = (state_rows.astype(F32) + rows_of(fwd_pieces)).astype(BF16)
    state_rows = from_behind(advanced, "section", 1)
    gain_total = gain_rows(gain0, 0) + gain_rows(gain1, 1)
    return (state_rows[None], grad_rows[None], gain_total[None])


def solution(mesh):
    in_specs = (
        P("section", ("dp", "tensor"), None),
        P("section", ("dp", "tensor"), None),
        P("section", None, ("dp", "tensor"), None),
        P("section", None, None),
        P("section", None, "dp", "tensor"),
        P("section", None, "dp", "tensor"),
        P("section", None, "dp", "tensor"),
        P("section", None, "tensor", "dp"),
        P(None, "dp", None),
        P(None, "dp", None),
    )
    out_specs = (
        P("section", ("dp", "tensor"), None),
        P("section", ("dp", "tensor"), None),
        P("section", None, None),
    )
    return jax.shard_map(
        per_device, mesh=mesh, in_specs=in_specs, out_specs=out_specs, check_vma=False
    )
```

```python
import functools
import math

import jax
import jax.numpy as jnp
from jax import lax
from jax.experimental import pallas as pl
from jax.experimental.pallas import tpu as pltpu
from jax.sharding import PartitionSpec as P

HD = 128
TICKS = 2
ROPE_BASE = 1000000.0
MESH = pl.DeviceIdType.MESH
F32 = jnp.float32
BF16 = jnp.bfloat16

WIDE = ("out", "all")


def exchange_kernel(kinds, n_dp, n_tensor, *refs):
    count = len(kinds)
    sources, targets = refs[:count], refs[count : 2 * count]
    send_sem, recv_sem, up_sem, down_sem, local_sem = refs[2 * count :]
    my_dp, my_tensor = lax.axis_index("dp"), lax.axis_index("tensor")
    n_all = n_dp * n_tensor
    me = my_dp * n_tensor + my_tensor
    order = sorted(range(count), key=lambda job: ("in", "out", "all", "rs", "ag").index(kinds[job]))
    flowing = [job for job in order if kinds[job] == "in"]

    def wide_peer(step):
        peer = lax.rem(me + step, n_all)
        return peer // n_tensor, lax.rem(peer, n_tensor)

    def narrow_peer(step):
        return lax.rem(my_dp + step, n_dp), my_tensor

    barrier = pltpu.get_barrier_semaphore()
    wide = any(kind in WIDE + ("in",) for kind in kinds)
    total = n_all if wide else n_dp
    pick = wide_peer if wide else narrow_peer

    @pl.loop(1, total)
    def greet(step):
        peer_dp, peer_tensor = pick(step)
        pl.semaphore_signal(
            barrier, inc=1, device_id={"dp": peer_dp, "tensor": peer_tensor}, device_id_type=MESH
        )

    pl.semaphore_wait(barrier, total - 1)

    def block(job, peer_dp, peer_tensor):
        kind = kinds[job]
        if kind in ("ag", "all"):
            return sources[job]
        if kind == "out":
            return sources[job].at[peer_dp, peer_tensor]
        return sources[job].at[peer_dp]

    def place(job):
        if kinds[job] in WIDE + ("in",):
            return targets[job].at[my_dp, my_tensor]
        return targets[job].at[my_dp]

    def steps(job):
        return n_all if kinds[job] in WIDE else n_dp

    def remote(job, step):
        peer_dp, peer_tensor = wide_peer(step) if kinds[job] in WIDE else narrow_peer(step)
        return pltpu.make_async_remote_copy(
            src_ref=block(job, peer_dp, peer_tensor),
            dst_ref=place(job),
            send_sem=send_sem.at[job, step],
            recv_sem=recv_sem.at[job, step],
            device_id={"dp": peer_dp, "tensor": peer_tensor},
            device_id_type=MESH,
        )

    def local(job):
        return pltpu.make_async_copy(block(job, my_dp, my_tensor), place(job), local_sem.at[job])

    def hop(job, step, source, move):
        owner = lax.rem(my_dp + n_dp - step, n_dp)
        sems = up_sem if move == 1 else down_sem
        return pltpu.make_async_remote_copy(
            src_ref=targets[job].at[owner, source],
            dst_ref=targets[job].at[owner, source],
            send_sem=sems.at[0, job, step, source],
            recv_sem=sems.at[1, job, step, source],
            device_id={"dp": my_dp, "tensor": lax.rem(my_tensor + move + n_tensor, n_tensor)},
            device_id_type=MESH,
        )

    for job in order:

        @pl.loop(1, steps(job))
        def send(step, job=job):
            remote(job, step).start()

    for job in order:
        local(job).start()
    for job in order:
        local(job).wait()

    def pass_on(job, step, source):
        @pl.when((source <= my_tensor) & (my_tensor < n_tensor - 1))
        def up():
            hop(job, step, source, 1).start()

        @pl.when((source >= my_tensor) & (my_tensor > 0))
        def down():
            hop(job, step, source, -1).start()

    for job in flowing:
        pass_on(job, 0, my_tensor)

        @pl.loop(1, n_dp)
        def first(step, job=job):
            remote(job, step).wait_recv()
            pass_on(job, step, my_tensor)

    for job in flowing:

        @pl.loop(1, n_tensor)
        def onward(distance, job=job):
            below, above = my_tensor - distance, my_tensor + distance

            @pl.loop(0, n_dp)
            def piece(step):
                @pl.when(below >= 0)
                def from_below():
                    hop(job, step, below, 1).wait_recv()
                    pass_on(job, step, below)

                @pl.when(above < n_tensor)
                def from_above():
                    hop(job, step, above, -1).wait_recv()
                    pass_on(job, step, above)

    for job in flowing:

        @pl.loop(1, n_dp)
        def sent(step, job=job):
            remote(job, step).wait_send()

        @pl.loop(0, n_tensor)
        def handed(source, job=job):
            @pl.loop(0, n_dp)
            def piece(step):
                @pl.when((source <= my_tensor) & (my_tensor < n_tensor - 1))
                def up():
                    hop(job, step, source, 1).wait_send()

                @pl.when((source >= my_tensor) & (my_tensor > 0))
                def down():
                    hop(job, step, source, -1).wait_send()

    for job in order:
        if job not in flowing:

            @pl.loop(1, steps(job))
            def finish(step, job=job):
                remote(job, step).wait()


def exchange(collective_id, *jobs):
    n_dp, n_tensor = lax.axis_size("dp"), lax.axis_size("tensor")
    kinds = tuple(kind for kind, _ in jobs)
    arrays = [value for _, value in jobs]
    shapes = []
    for kind, value in jobs:
        lead = {
            "in": (n_dp, n_tensor) + value.shape[1:],
            "out": value.shape,
            "all": (n_dp, n_tensor) + value.shape,
            "rs": value.shape,
            "ag": (n_dp,) + value.shape,
        }[kind]
        shapes.append(jax.ShapeDtypeStruct(lead, value.dtype))
    count = len(jobs)
    most = n_dp * n_tensor
    return pl.pallas_call(
        functools.partial(exchange_kernel, kinds, n_dp, n_tensor),
        out_shape=shapes,
        in_specs=[pl.BlockSpec(memory_space=pl.ANY)] * count,
        out_specs=[pl.BlockSpec(memory_space=pl.ANY)] * count,
        scratch_shapes=[
            pltpu.SemaphoreType.DMA((count, most)),
            pltpu.SemaphoreType.DMA((count, most)),
            pltpu.SemaphoreType.DMA((2, count, n_dp, n_tensor)),
            pltpu.SemaphoreType.DMA((2, count, n_dp, n_tensor)),
            pltpu.SemaphoreType.DMA((count,)),
        ],
        compiler_params=pltpu.CompilerParams(
            collective_id=collective_id, has_side_effects=True
        ),
        name="exchange_" + "_".join(kinds),
    )(*arrays)


def from_behind(value, axis, steps):
    count = lax.axis_size(axis)
    pairs = [(source, (source + steps) % count) for source in range(count)]
    return lax.ppermute(value, axis, pairs)


def rope_tables(segments):
    count_rows = segments.shape[1]
    row_index = jnp.arange(count_rows, dtype=jnp.int32)
    allowed = (segments[:, :, None] == segments[:, None, :]) & (
        row_index[:, None] >= row_index[None, :]
    )[None]
    allowed = allowed.astype(F32)
    positions = jnp.sum(allowed, axis=2) - 1.0
    halfway = HD // 2
    frequency = jnp.exp(jnp.arange(halfway, dtype=F32) * (-2.0 * math.log(ROPE_BASE) / HD))
    angles = positions[:, :, None] * frequency
    cosine, sine = jnp.cos(angles), jnp.sin(angles)
    return (
        jnp.concatenate([cosine, cosine], axis=2),
        jnp.concatenate([-sine, sine], axis=2),
        allowed,
    )


def dot(left, right, contract):
    return lax.dot_general(left, right, (contract, ((), ())), preferred_element_type=F32)


ROWS_COLUMNS, COLUMNS_COLUMNS, ROWS_ROWS = ((1,), (0,)), ((1,), (1,)), ((0,), (0,))


def total(pieces, first):
    value = pieces[0, :, first : first + HD].astype(F32)
    for index in range(1, pieces.shape[0]):
        value = value + pieces[index, :, first : first + HD].astype(F32)
    return value


def turn(value, cosine, sine):
    return value * cosine + pltpu.roll(value, HD // 2, 1) * sine


def softmax(query, key, allowed):
    scores = dot(query, key, COLUMNS_COLUMNS) * (1.0 / math.sqrt(HD))
    exponents = jnp.exp(jnp.where(allowed > 0.5, scores, -1e30))
    return exponents / jnp.sum(exponents, axis=1, keepdims=True)


def attention_kernel(widths, pieces, cosine, sine, allowed, mixed):
    query_width, key_width = widths
    group = query_width // key_width
    cos, sin, keep = cosine[...], sine[...], allowed[...]
    for key_head in range(key_width // HD):
        key = turn(total(pieces, query_width + key_head * HD), cos, sin).astype(BF16)
        value = total(pieces, query_width + key_width + key_head * HD).astype(BF16)
        for head in range(key_head * group, (key_head + 1) * group):
            query = turn(total(pieces, head * HD), cos, sin).astype(BF16)
            probs = softmax(query, key, keep).astype(BF16)
            mixed[:, head * HD : (head + 1) * HD] = dot(probs, value, ROWS_COLUMNS).astype(BF16)


def attention_gradient_kernel(widths, pieces, grads, cosine, sine, allowed, gradient):
    query_width, key_width = widths
    group = query_width // key_width
    cos, sin, keep = cosine[...], sine[...], allowed[...]
    for key_head in range(key_width // HD):
        key_at = query_width + key_head * HD
        value_at = key_at + key_width
        key = turn(total(pieces, key_at), cos, sin).astype(BF16)
        value = total(pieces, value_at).astype(BF16)
        key_grad = jnp.zeros(key.shape, F32)
        value_grad = jnp.zeros(key.shape, F32)
        for head in range(key_head * group, (key_head + 1) * group):
            query = turn(total(pieces, head * HD), cos, sin).astype(BF16)
            mixed_grad = total(grads, head * HD).astype(BF16)
            probs = softmax(query, key, keep)
            value_grad = value_grad + dot(probs.astype(BF16), mixed_grad, ROWS_ROWS)
            probs_grad = dot(mixed_grad, value, COLUMNS_COLUMNS).astype(BF16).astype(F32)
            mean = jnp.sum(probs_grad * probs, axis=1, keepdims=True)
            scores_grad = (probs * (probs_grad - mean) * (1.0 / math.sqrt(HD))).astype(BF16)
            query_grad = dot(scores_grad, key, ROWS_COLUMNS).astype(BF16).astype(F32)
            gradient[:, head * HD : (head + 1) * HD] = turn(query_grad, cos, -sin).astype(BF16)
            key_grad = key_grad + dot(scores_grad, query, ROWS_ROWS)
        key_grad = key_grad.astype(BF16).astype(F32)
        gradient[:, key_at : key_at + HD] = turn(key_grad, cos, -sin).astype(BF16)
        gradient[:, value_at : value_at + HD] = value_grad.astype(BF16)


def in_vmem(kernel, widths, out_width, *operands):
    count_rows = operands[0].shape[1]
    return pl.pallas_call(
        functools.partial(kernel, widths),
        out_shape=jax.ShapeDtypeStruct((count_rows, out_width), BF16),
        in_specs=[pl.BlockSpec(memory_space=pltpu.VMEM)] * len(operands),
        out_specs=pl.BlockSpec(memory_space=pltpu.VMEM),
        compiler_params=pltpu.CompilerParams(vmem_limit_bytes=32 * 1024 * 1024),
    )(*operands)


def normalise(rows, gain_vector):
    variance = jnp.mean(rows * rows, axis=1, keepdims=True)
    return rows * lax.rsqrt(variance + 1e-06) * gain_vector


def pick_span(table, span):
    return lax.dynamic_index_in_dim(table, span, 0, keepdims=False)


def dot_t(left, right):
    return lax.dot_general(left, right, (((1,), (1,)), ((), ())), preferred_element_type=F32)


def per_device(
    fwd_state, bwd_state, stash, gains, w_query, w_key, w_value, w_out, fwd_segments, bwd_segments
):
    n_dp, n_tensor = lax.axis_size("dp"), lax.axis_size("tensor")
    phase_count = lax.axis_size("section")
    phase_index = lax.axis_index("section")
    own_rows, model_width = fwd_state.shape[1:]
    part = model_width // n_dp
    replica_rows = own_rows * n_tensor
    all_rows = replica_rows * n_dp
    widths = (w_query.shape[3], w_key.shape[3])

    def columns(rows):
        return rows.reshape(own_rows, n_dp, part).transpose(1, 0, 2)

    def project(normed, span):
        normed = normed.reshape(all_rows, part)
        pieces = [
            jnp.dot(normed, pick_span(weight[0], span), preferred_element_type=F32).astype(BF16)
            for weight in (w_query, w_key, w_value)
        ]
        return jnp.concatenate(pieces, axis=1).reshape(n_dp, replica_rows, -1)

    def to_owners(term):
        return term.astype(BF16).reshape(n_dp, n_tensor, own_rows, part)

    def rows_of(pieces):
        return jnp.sum(pieces.astype(F32), axis=1).transpose(1, 0, 2).reshape(own_rows, model_width)

    gains32 = gains[0].astype(F32)
    my_part = lax.dynamic_slice_in_dim(gains32, lax.axis_index("dp") * part, part, axis=1)
    stash32 = stash[0].astype(F32)
    fwd_spans = [jnp.where(phase_index < tick, 1, 0).astype(jnp.int32) for tick in range(TICKS)]
    bwd_spans = [
        jnp.where(phase_index > phase_count - 1 - tick, 0, 1).astype(jnp.int32)
        for tick in range(TICKS)
    ]
    rows_ids = [
        pick_span(fwd_segments[:, 0], (phase_index - tick) % phase_count) for tick in range(TICKS)
    ] + [pick_span(bwd_segments[:, 0], (phase_index + tick) % phase_count) for tick in range(TICKS)]
    tables = rope_tables(jnp.stack(rows_ids))

    def attention(projected, tick):
        return in_vmem(
            attention_kernel, widths, widths[0], projected, *[table[tick] for table in tables]
        )

    def forward_in(state_rows, tick):
        gain = pick_span(gains32, fwd_spans[tick])
        return columns(normalise(state_rows.astype(F32), gain).astype(BF16))

    def stash_in(tick):
        gain = pick_span(gains32, bwd_spans[tick])
        return columns(normalise(stash32[tick], gain).astype(BF16))

    def forward_out(mixed, tick):
        mixed = mixed.reshape(all_rows, -1)
        return to_owners(
            jnp.dot(mixed, pick_span(w_out[0], fwd_spans[tick]), preferred_element_type=F32)
        )

    def mixed_gradient(grad, tick):
        grad = grad.reshape(all_rows, part)
        return (
            dot_t(grad, pick_span(w_out[0], bwd_spans[tick]))
            .astype(BF16)
            .reshape(n_dp, replica_rows, -1)
        )

    def attention_gradient(projected, mixed_grad, tick):
        return in_vmem(
            attention_gradient_kernel,
            widths,
            widths[0] + 2 * widths[1],
            projected,
            mixed_grad,
            *[table[TICKS + tick] for table in tables],
        )

    def normed_gradient(gradient, normed, tick):
        gradient = gradient.reshape(all_rows, -1)
        span = bwd_spans[tick]
        query_width, key_width = widths
        term = (
            dot_t(gradient[:, :query_width], pick_span(w_query[0], span))
            + dot_t(gradient[:, query_width : query_width + key_width], pick_span(w_key[0], span))
            + dot_t(gradient[:, query_width + key_width :], pick_span(w_value[0], span))
        )
        gain_term = jnp.sum(term * normed.reshape(all_rows, part).astype(F32), axis=0)
        gain_term = gain_term / pick_span(my_part, span)
        return to_owners(term), gain_term.reshape(-1, 128)

    def returned_rows(grad_rows, pieces, tick):
        gain = pick_span(gains32, bwd_spans[tick])
        _, pull = jax.vjp(lambda rows: normalise(rows, gain), stash32[tick])
        return (grad_rows.astype(F32) + pull(rows_of(pieces))[0]).astype(BF16)

    span_ids = jnp.arange(2, dtype=jnp.int32)

    def gain_rows(pieces, tick):
        gain = jnp.sum(pieces, axis=1).reshape(model_width)
        chosen = (span_ids == bwd_spans[tick]).astype(F32)
        return chosen[:, None] * gain[None, :]

    state_rows, grad_rows = fwd_state[0], bwd_state[0]
    stash0, state = exchange(0, ("in", stash_in(0)), ("in", forward_in(state_rows, 0)))
    grad, bwd_proj, fwd_proj = exchange(
        1,
        ("in", columns(grad_rows)),
        ("rs", project(stash0, bwd_spans[0])),
        ("rs", project(state, fwd_spans[0])),
    )
    stash1, mixed_grad, mixed = exchange(
        2,
        ("in", stash_in(1)),
        ("rs", mixed_gradient(grad, 0)),
        ("ag", attention(fwd_proj, 0)),
    )
    gradient = attention_gradient(bwd_proj, mixed_grad, 0)
    fwd_pieces, gradient = exchange(3, ("out", forward_out(mixed, 0)), ("ag", gradient))
    advanced = (state_rows.astype(F32) + rows_of(fwd_pieces)).astype(BF16)
    state_rows = from_behind(advanced, "section", 1)
    term, gain_term = normed_gradient(gradient, stash0, 0)
    bwd_pieces, gain0, state, bwd_proj = exchange(
        4,
        ("out", term),
        ("all", gain_term),
        ("in", forward_in(state_rows, 1)),
        ("rs", project(stash1, bwd_spans[1])),
    )
    grad_rows = from_behind(returned_rows(grad_rows, bwd_pieces, 0), "section", -1)
    grad, fwd_proj = exchange(
        5, ("in", columns(grad_rows)), ("rs", project(state, fwd_spans[1]))
    )
    mixed_grad, mixed = exchange(
        6, ("rs", mixed_gradient(grad, 1)), ("ag", attention(fwd_proj, 1))
    )
    gradient = attention_gradient(bwd_proj, mixed_grad, 1)
    fwd_pieces, gradient = exchange(7, ("out", forward_out(mixed, 1)), ("ag", gradient))
    advanced = (state_rows.astype(F32) + rows_of(fwd_pieces)).astype(BF16)
    state_rows = from_behind(advanced, "section", 1)
    term, gain_term = normed_gradient(gradient, stash1, 1)
    bwd_pieces, gain1 = exchange(8, ("out", term), ("all", gain_term))
    grad_rows = from_behind(returned_rows(grad_rows, bwd_pieces, 1), "section", -1)
    gain_total = gain_rows(gain0, 0) + gain_rows(gain1, 1)
    return (state_rows[None], grad_rows[None], gain_total[None])


def solution(mesh):
    in_specs = (
        P("section", ("dp", "tensor"), None),
        P("section", ("dp", "tensor"), None),
        P("section", None, ("dp", "tensor"), None),
        P("section", None, None),
        P("section", None, "dp", "tensor"),
        P("section", None, "dp", "tensor"),
        P("section", None, "dp", "tensor"),
        P("section", None, "tensor", "dp"),
        P(None, "dp", None),
        P(None, "dp", None),
    )
    out_specs = (
        P("section", ("dp", "tensor"), None),
        P("section", ("dp", "tensor"), None),
        P("section", None, None),
    )
    return jax.shard_map(
        per_device, mesh=mesh, in_specs=in_specs, out_specs=out_specs, check_vma=False
    )
```
